32 devices in a mesh: parts: 2 (over x), row: 16 (over z, y, core).
Axes of the slice: x: 2, y: 2, z: 4, core: 2. Of those that a mesh axis runs over, the one named last changes fastest.
Arguments:
- z_left: bfloat16 [512, 256, 128], P(('parts', 'row')), parts along dimension 0, may hold values from -6 to 6
- z_right: bfloat16 [128, 256, 128], P(('parts', 'row')), parts along dimension 0, may hold values from -6 to 6
- pair_block: bfloat16 [512, 64, 128], P('parts', 'row'), parts along dimension 0, may hold values from -6 to 6
- row_valid: int32 [512], P(('parts', 'row')), parts along dimension 0, may hold values 0 or 1
- col_valid: int32 [128], P(('parts', 'row')), parts along dimension 0, may hold values 0 or 1
- k_valid: int32 [512], P('parts'), parts along dimension 0, may hold values 0 or 1
- in_gain: float32 [128], replicated, may hold values from 0.1 to 1.9
- w_left: bfloat16 [128, 256], replicated, may hold values from -0.5 to 0.5
- w_right: bfloat16 [128, 256], replicated, may hold values from -0.5 to 0.5
- w_gate: bfloat16 [128, 128], replicated, may hold values from -0.5 to 0.5
- w_out: bfloat16 [128, 128], replicated, may hold values from -0.5 to 0.5
- out_gain: float32 [128], replicated, may hold values from 0.1 to 1.9
Outputs:
- update: bfloat16 [512, 64, 128], P('parts', 'row'), parts along dimension 0
The draws below stay inside these ranges and needn't reach their ends.
There are 2 independent parts, one for each index of `parts`. The reference program is written for one: setup_inputs(seed, part) draws one part's arguments, and reference() takes and returns one part's arrays. A program takes and returns all parts, laid end to end along the dimension named above; an argument that names none is the same for every part. Nothing has to cross between parts.
All inputs are finite; a program needn't handle non-finite values. No bound on the sum of `row_valid` or of `col_valid` on one device may be relied on, other than what follows from the above.
Results may differ from the reference program's by a relative error of at most 0.0081.
Values may be sent and summed in bfloat16 or wider, within the bound.
A program may use at most 320 MiB of HBM per device.

```python
import jax
import jax.numpy as jnp
from jax import lax

C = 128
CH = 128
ROWS = 256
KW = 256
COLS = 64


def with_ends(result, own_key, low, largest):
    place = [jax.random.randint(jax.random.fold_in(own_key, axis), (), 0, length) for axis, length in enumerate(result.shape)]
    main_axis = result.shape.index(max(result.shape))
    neighbour = place[:main_axis] + [(place[main_axis] + 1) % result.shape[main_axis]] + place[main_axis + 1:]
    return result.at[tuple(place)].set(low).at[tuple(neighbour)].set(largest)


def level_of(stream_key, extent, shards, low, largest):
    loudness, own = 1.0, jax.random.fold_in(stream_key, 6)
    for axis_at, shards_of in shards:
        heights = jnp.exp(jax.random.uniform(jax.random.fold_in(own, axis_at), (shards_of,), jnp.float32, low / len(shards), largest / len(shards)))
        loudness = loudness * jnp.repeat(heights, extent[axis_at] // shards_of).reshape([-1 if axis == axis_at else 1 for axis in range(len(extent))])
    return loudness


def bell_draw(rng, shape, deviation, most, pieces=(), held_as=jnp.bfloat16):
    array = deviation * jax.random.normal(rng, shape, jnp.float32)
    if pieces:
        array = array * level_of(rng, shape, pieces, -0.22, 0.18)
    return jnp.clip(array, -most, most).astype(held_as)


def setup_inputs(seed: int = 0, part: int = 0) -> dict:
    key_of = jax.random.split(jax.random.key(seed), 13)
    own_keys = jax.random.split(jax.random.fold_in(key_of[12], part), 13)
    return {
        "z_left": bell_draw(own_keys[0], (ROWS, KW, C), 1.0, 6.0, ((0, 16),)),
        "z_right": bell_draw(own_keys[1], (COLS, KW, C), 1.0, 6.0, ((0, 16),)),
        "pair_block": bell_draw(own_keys[2], (ROWS, COLS, C), 1.0, 6.0, ((1, 16),)),
        "row_valid": with_ends((jax.random.randint(own_keys[3], (ROWS,), 0, 8) < 7).astype(jnp.int32), jax.random.fold_in(own_keys[3], 1), 0, 1),
        "col_valid": with_ends((jax.random.randint(own_keys[4], (COLS,), 0, 8) < 7).astype(jnp.int32), jax.random.fold_in(own_keys[4], 1), 0, 1),
        "k_valid": with_ends((jax.random.randint(own_keys[5], (KW,), 0, 8) < 7).astype(jnp.int32), jax.random.fold_in(own_keys[5], 1), 0, 1),
        "in_gain": jnp.clip(1.0 + 0.18 * jax.random.normal(key_of[6], (C,), jnp.float32), 0.1, 1.9),
        "w_left": bell_draw(key_of[7], (C, 2 * CH), C ** -0.5, 0.5),
        "w_right": bell_draw(key_of[8], (C, 2 * CH), C ** -0.5, 0.5),
        "w_gate": bell_draw(key_of[9], (C, C), C ** -0.5, 0.5),
        "w_out": bell_draw(key_of[10], (CH, C), CH ** -0.5, 0.5),
        "out_gain": jnp.clip(1.0 + 0.18 * jax.random.normal(key_of[11], (CH,), jnp.float32), 0.1, 1.9),
    }


def layer_norm(values, scale_gain):
    average = lax.optimization_barrier(jnp.mean(values, axis=-1, keepdims=True))
    centered = values - average
    variance = lax.optimization_barrier(jnp.mean(centered * centered, axis=-1, keepdims=True))
    return centered / jnp.sqrt(variance + 1e-05) * scale_gain

def activations(raw_pairs, valid_rows, k_valid, in_gain, weight):
    k_mask = k_valid.astype(jnp.float32)

    def one_row(item):
        raw_row, valid_one = item
        normed = layer_norm(raw_row.astype(jnp.float32), in_gain).astype(jnp.bfloat16)
        projected = jnp.dot(normed, weight, preferred_element_type=jnp.float32)
        hidden = projected.shape[-1] // 2
        masking = valid_one.astype(jnp.float32) * k_mask
        return (jax.nn.sigmoid(projected[:, :hidden]) * projected[:, hidden:] * masking[:, None]).astype(jnp.bfloat16)
    return lax.map(one_row, (raw_pairs, valid_rows))

def reference(z_left, z_right, pair_block, row_valid, col_valid, k_valid, in_gain, w_left, w_right, w_gate, w_out, out_gain):
    left_act = activations(z_left, row_valid, k_valid, in_gain, w_left)
    right_act = activations(z_right, col_valid, k_valid, in_gain, w_right)
    triangle = jnp.einsum('ikc,jkc->ijc', left_act.astype(jnp.float32), right_act.astype(jnp.float32))
    tnorm = layer_norm(triangle, out_gain).astype(jnp.bfloat16)
    row_count, col_count, channels = pair_block.shape
    normed_block = layer_norm(pair_block.astype(jnp.float32), in_gain).astype(jnp.bfloat16)
    gate_value = jax.nn.sigmoid(jnp.dot(normed_block.reshape(-1, channels), w_gate, preferred_element_type=jnp.float32))
    outward = jnp.dot(tnorm.reshape(-1, tnorm.shape[-1]), w_out, preferred_element_type=jnp.float32)
    return (gate_value * outward).reshape(row_count, col_count, channels).astype(jnp.bfloat16)
```

```python
import functools

import jax
import jax.numpy as jnp
from jax import lax
from jax.experimental import pallas as pl
from jax.experimental.pallas import tpu as pltpu
from jax.sharding import PartitionSpec as P

MESH = pl.DeviceIdType.MESH
F32 = jnp.float32
BF16 = jnp.bfloat16


def layer_norm(values, scale_gain):
    average = jnp.mean(values, axis=-1, keepdims=True)
    centered = values - average
    variance = jnp.mean(centered * centered, axis=-1, keepdims=True)
    return centered / jnp.sqrt(variance + 1e-05) * scale_gain


def activations(raw_pairs, valid_rows, k_valid, in_gain, weight):
    row_count, width_k, channels = raw_pairs.shape
    normed = layer_norm(raw_pairs.astype(F32), in_gain).astype(BF16)
    projected = jnp.dot(
        normed.reshape(row_count * width_k, channels), weight, preferred_element_type=F32
    )
    projected = projected.reshape(row_count, width_k, -1)
    hidden = projected.shape[-1] // 2
    masking = valid_rows.astype(F32)[:, None] * k_valid.astype(F32)[None, :]
    return (
        jax.nn.sigmoid(projected[..., :hidden]) * projected[..., hidden:] * masking[..., None]
    ).astype(BF16)


def local_collectives(
    z_left, z_right, pair_block, row_valid, col_valid, k_valid,
    in_gain, w_left, w_right, w_gate, w_out, out_gain,
):
    left_act = activations(z_left, row_valid, k_valid, in_gain, w_left)
    right_act = activations(z_right, col_valid, k_valid, in_gain, w_right)
    hidden = left_act.shape[2]
    block_rows, block_cols, channels = pair_block.shape
    triangle = jnp.einsum(
        "ikc,jkc->ijc",
        left_act,
        lax.all_gather(right_act, "row", axis=0, tiled=True),
        preferred_element_type=F32,
    )
    tnorm = layer_norm(triangle, out_gain).astype(BF16)
    swapped = lax.all_to_all(tnorm, "row", split_axis=1, concat_axis=0, tiled=True)
    normed_block = layer_norm(pair_block.astype(F32), in_gain).astype(BF16)
    gate_value = jax.nn.sigmoid(
        jnp.dot(normed_block.reshape(-1, channels), w_gate, preferred_element_type=F32)
    )
    outward = jnp.dot(swapped.reshape(-1, hidden), w_out, preferred_element_type=F32)
    return (gate_value * outward).reshape(block_rows, block_cols, channels).astype(BF16)


def sigmoid(value):
    return 0.5 * jnp.tanh(0.5 * value) + 0.5


def normed_rows(raw, gain, averaging):
    centered = raw.astype(F32) - jnp.dot(raw, averaging, preferred_element_type=F32)
    variance = jnp.dot((centered * centered).astype(BF16), averaging, preferred_element_type=F32)
    return (centered * lax.rsqrt(variance + 1e-05) * gain).astype(BF16)


def kernel(
    n,
    z_left, z_right, pair, row_valid, col_valid, k_valid, in_gain, w_left, w_right, w_gate, w_out, out_gain,
    out,
    gathered, left, gate, band, partial, outgoing, incoming,
    got, up_sem, down_sem, side_sem, twin_sem, back_sem, back_got,
):
    rows, width, channels = z_left.shape
    cols = z_right.shape[0]
    per_block = rows * cols
    nz = n // 4
    me = lax.axis_index("row")
    core = lax.rem(me, 2)
    y = lax.rem(me // 2, 2)
    z = me // 4

    def place(pz, py, pc):
        return (pz * 2 + py) * 2 + pc

    barrier = pltpu.get_barrier_semaphore()

    def greet(step, _):
        peer = lax.rem(me + step, n)
        pl.semaphore_signal(barrier, inc=1, device_id={"row": peer}, device_id_type=MESH)
        return 0

    lax.fori_loop(1, n, greet, 0)

    def carry(src, chunk, sem, target):
        return pltpu.make_async_remote_copy(
            src_ref=gathered.at[src, chunk],
            dst_ref=gathered.at[src, chunk],
            send_sem=sem,
            recv_sem=got.at[src, chunk],
            device_id={"row": target},
            device_id_type=MESH,
        )

    def go_up(pz, chunk):
        return carry(place(pz, y, core), chunk, up_sem.at[pz, chunk], lax.rem(me + 4, n))

    def go_down(pz, chunk):
        return carry(place(pz, y, core), chunk, down_sem.at[pz, chunk], lax.rem(me + n - 4, n))

    def go_side(pz, chunk):
        return carry(place(pz, y, core), chunk, side_sem.at[pz, chunk], place(z, 1 - y, core))

    def go_twin(pz, py, chunk):
        return carry(
            place(pz, py, core), chunk, twin_sem.at[pz * 2 + py, chunk], place(z, y, 1 - core)
        )

    def give_back(src):
        return pltpu.make_async_remote_copy(
            src_ref=outgoing.at[src],
            dst_ref=incoming.at[me],
            send_sem=back_sem.at[src],
            recv_sem=back_got.at[me],
            device_id={"row": src},
            device_id_type=MESH,
        )

    def wait_got(src, chunk):
        carry(src, chunk, up_sem.at[0, 0], place(z, y, 1 - core)).wait_recv()

    averaging = jnp.full((channels, channels), 1.0 / channels, BF16)
    gain = in_gain[...]

    across = lax.broadcasted_iota(jnp.int32, (width, width), 0)
    along = lax.broadcasted_iota(jnp.int32, (width, width), 1)
    spread = jnp.where(across == along, k_valid[...].astype(F32), 0.0).astype(BF16)
    k_mask = jnp.dot(spread, jnp.ones((width, channels), BF16), preferred_element_type=F32)

    for chunk in range(cols):
        projected = jnp.dot(
            normed_rows(z_right[chunk], gain, averaging), w_right[...], preferred_element_type=F32
        )
        valid = col_valid[chunk].astype(F32)
        gathered[me, chunk] = (
            sigmoid(projected[:, :channels]) * projected[:, channels:] * (k_mask * valid)
        ).astype(BF16)
        if chunk == 0:
            pl.semaphore_wait(barrier, n - 1)

        @pl.when(z + 1 < nz)
        def _():
            go_up(z, chunk).start()

        @pl.when(z > 0)
        def _():
            go_down(z, chunk).start()

        go_side(z, chunk).start()
        go_twin(z, y, chunk).start()

    def left_rows(quarter):
        def one(step, _):
            i = quarter * (rows // cols) + step
            projected = jnp.dot(
                normed_rows(z_left[i], gain, averaging), w_left[...], preferred_element_type=F32
            )
            valid = row_valid[i].astype(F32)
            left[i] = (
                (sigmoid(projected[:, :channels]) * projected[:, channels:] * valid)
                .astype(BF16)
                .astype(F32)
            )
            return 0

        lax.fori_loop(0, rows // cols, one, 0)

    def gate_rows(quarter):
        size = pair.shape[0] // cols
        span = pl.ds(pl.multiple_of(quarter * size, size), size)
        normed = normed_rows(pair[span, :], gain, averaging)
        gate[span, :] = sigmoid(jnp.dot(normed, w_gate[...], preferred_element_type=F32))

    pick_row = lax.broadcasted_iota(jnp.int32, (per_block, per_block * 8), 0)
    pick_col = lax.broadcasted_iota(jnp.int32, (per_block, per_block * 8), 1)
    summing = (pick_col // 8 == pick_row).astype(BF16)
    group = 4

    def triangle_block(src):
        band[...] = gathered[src].astype(F32)

        def some_rows(at, _):
            def some_k(kk, totals):
                totals = list(totals)
                for part in range(4):
                    span = pl.ds(pl.multiple_of(kk * 32 + part * 8, 8), 8)
                    rights = [band[j, span, :] for j in range(cols)]
                    for ii in range(group):
                        one_left = left[at * group + ii, span, :]
                        for j in range(cols):
                            totals[ii * cols + j] = totals[ii * cols + j] + one_left * rights[j]
                return tuple(totals)

            totals = lax.fori_loop(
                0, width // 32, some_k,
                tuple(jnp.zeros((8, channels), F32) for _ in range(group * cols)),
            )
            for index, total in enumerate(totals):
                partial[pl.ds(pl.multiple_of((at * group * cols + index) * 8, 8), 8), :] = total
            return 0

        lax.fori_loop(0, rows // group, some_rows, 0)
        whole = partial[...]
        high = whole.astype(BF16)
        low = (whole - high.astype(F32)).astype(BF16)
        triangle = jnp.dot(summing, high, preferred_element_type=F32) + jnp.dot(
            summing, low, preferred_element_type=F32
        )
        centered = triangle - jnp.mean(triangle, axis=-1, keepdims=True)
        variance = jnp.mean(centered * centered, axis=-1, keepdims=True)
        tnorm = (centered * lax.rsqrt(variance + 1e-05) * out_gain[...]).astype(BF16)
        outward = jnp.dot(tnorm, w_out[...], preferred_element_type=F32).astype(BF16)

        @pl.when(src == me)
        def _():
            incoming[me] = outward

        @pl.when(src != me)
        def _():
            outgoing[src] = outward
            give_back(src).start()

    def step(t, _):
        distance = t // cols
        chunk = lax.rem(t, cols)

        def arrivals(way, _):
            sign = 1 - 2 * way
            pz = z + (distance + 1) * sign

            @pl.when((pz >= 0) & (pz < nz))
            def _():
                wait_got(place(pz, y, core), chunk)

                @pl.when((way == 0) & (z > 0))
                def _():
                    go_down(pz, chunk).start()

                @pl.when((way == 1) & (z + 1 < nz))
                def _():
                    go_up(pz, chunk).start()

                go_side(pz, chunk).start()
                go_twin(pz, y, chunk).start()

            qz = z + distance * sign

            @pl.when((qz >= 0) & (qz < nz) & ((distance > 0) | (way == 0)))
            def _():
                wait_got(place(qz, 1 - y, core), chunk)
                go_twin(qz, 1 - y, chunk).start()

            return 0

        lax.fori_loop(0, 2, arrivals, 0)

        @pl.when(distance == 0)
        def _():
            left_rows(chunk)

        @pl.when(distance == 1)
        def _():
            gate_rows(chunk)

        def blocks(way, _):
            before = distance - 1
            pz = z + before * (1 - 2 * way)
            across_y = lax.rem(chunk, 2)
            across_core = chunk // 2

            @pl.when((pz >= 0) & (pz < nz) & ((before > 0) | ((before == 0) & (way == 0))))
            def _():
                py = lax.rem(y + across_y, 2)
                src = place(pz, py, lax.rem(core + across_core, 2))

                @pl.when(across_core == 1)
                def _():
                    for c in range(cols):
                        wait_got(src, c)

                triangle_block(src)

            return 0

        lax.fori_loop(0, 2, blocks, 0)
        return 0

    lax.fori_loop(0, (nz + 1) * cols, step, 0)

    def finish(src, _):
        @pl.when(src != me)
        def _():
            pltpu.make_async_remote_copy(
                src_ref=outgoing.at[src],
                dst_ref=incoming.at[src],
                send_sem=back_sem.at[src],
                recv_sem=back_got.at[src],
                device_id={"row": src},
                device_id_type=MESH,
            ).wait_recv()

        span = pl.ds(pl.multiple_of(src * per_block, per_block), per_block)
        out[span, :] = (gate[span, :] * incoming[src].astype(F32)).astype(BF16)
        return 0

    lax.fori_loop(0, n, finish, 0)

    def settle(pz, _):
        for chunk in range(cols):
            @pl.when((pz <= z) & (z + 1 < nz))
            def _():
                go_up(pz, chunk).wait_send()

            @pl.when((pz >= z) & (z > 0))
            def _():
                go_down(pz, chunk).wait_send()

            go_side(pz, chunk).wait_send()
            go_twin(pz, 0, chunk).wait_send()
            go_twin(pz, 1, chunk).wait_send()
        return 0

    lax.fori_loop(0, nz, settle, 0)

    def settle_back(src, _):
        @pl.when(src != me)
        def _():
            give_back(src).wait_send()

        return 0

    lax.fori_loop(0, n, settle_back, 0)


def local_kernel(
    n,
    z_left, z_right, pair_block, row_valid, col_valid, k_valid,
    in_gain, w_left, w_right, w_gate, w_out, out_gain,
):
    rows, width, channels = z_left.shape
    cols = z_right.shape[0]
    per_block = rows * cols
    vmem = pl.BlockSpec(memory_space=pltpu.VMEM)
    smem = pl.BlockSpec(memory_space=pltpu.SMEM)
    nz = n // 4
    dma = pltpu.SemaphoreType.DMA
    flat = pl.pallas_call(
        functools.partial(kernel, n),
        out_shape=jax.ShapeDtypeStruct((n * per_block, channels), BF16),
        in_specs=[vmem, vmem, vmem, smem, smem] + [vmem] * 7,
        out_specs=vmem,
        scratch_shapes=[
            pltpu.VMEM((n, cols, width, channels), BF16),
            pltpu.VMEM((rows, width, channels), F32),
            pltpu.VMEM((n * per_block, channels), F32),
            pltpu.VMEM((cols, width, channels), F32),
            pltpu.VMEM((per_block * 8, channels), F32),
            pltpu.VMEM((n, per_block, channels), BF16),
            pltpu.VMEM((n, per_block, channels), BF16),
            dma((n, cols)),
            dma((nz, cols)),
            dma((nz, cols)),
            dma((nz, cols)),
            dma((nz * 2, cols)),
            dma((n,)),
            dma((n,)),
        ],
        compiler_params=pltpu.CompilerParams(
            collective_id=0, has_side_effects=True, vmem_limit_bytes=40 * 1024 * 1024
        ),
    )(
        z_left, z_right, pair_block.reshape(-1, channels), row_valid, col_valid,
        k_valid.reshape(1, -1), in_gain.reshape(1, -1), w_left, w_right, w_gate, w_out,
        out_gain.reshape(1, -1),
    )
    return flat.reshape(pair_block.shape)


def fits(n, z_left, z_right):
    rows, width, channels = z_left.shape
    cols = z_right.shape[0]
    return (
        n % 4 == 0
        and cols == 4
        and rows % 4 == 0
        and width % 32 == 0
        and n * cols * width * channels * 2 <= 8 * 1024 * 1024
    )


def solution(mesh):
    n = mesh.shape["row"]

    def local(*arrays):
        if fits(n, arrays[0], arrays[1]):
            return local_kernel(n, *arrays)
        return local_collectives(*arrays)

    placed = (
        P(("parts", "row"), None, None),
        P(("parts", "row"), None, None),
        P("parts", "row", None),
        P(("parts", "row")),
        P(("parts", "row")),
        P("parts"),
        P(),
        P(),
        P(),
        P(),
        P(),
        P(),
    )
    return jax.shard_map(
        local, mesh=mesh, in_specs=placed, out_specs=P("parts", "row", None), check_vma=False
    )
```

```python
import functools

import jax
import jax.numpy as jnp
from jax import lax
from jax.experimental import pallas as pl
from jax.experimental.pallas import tpu as pltpu
from jax.sharding import PartitionSpec as P

MESH = pl.DeviceIdType.MESH
F32 = jnp.float32
BF16 = jnp.bfloat16


def layer_norm(values, scale_gain):
    average = jnp.mean(values, axis=-1, keepdims=True)
    centered = values - average
    variance = jnp.mean(centered * centered, axis=-1, keepdims=True)
    return centered / jnp.sqrt(variance + 1e-05) * scale_gain


def activations(raw_pairs, valid_rows, k_valid, in_gain, weight):
    row_count, width_k, channels = raw_pairs.shape
    normed = layer_norm(raw_pairs.astype(F32), in_gain).astype(BF16)
    projected = jnp.dot(
        normed.reshape(row_count * width_k, channels), weight, preferred_element_type=F32
    )
    projected = projected.reshape(row_count, width_k, -1)
    hidden = projected.shape[-1] // 2
    masking = valid_rows.astype(F32)[:, None] * k_valid.astype(F32)[None, :]
    return (
        jax.nn.sigmoid(projected[..., :hidden]) * projected[..., hidden:] * masking[..., None]
    ).astype(BF16)


def local_collectives(
    z_left, z_right, pair_block, row_valid, col_valid, k_valid,
    in_gain, w_left, w_right, w_gate, w_out, out_gain,
):
    left_act = activations(z_left, row_valid, k_valid, in_gain, w_left)
    right_act = activations(z_right, col_valid, k_valid, in_gain, w_right)
    hidden = left_act.shape[2]
    block_rows, block_cols, channels = pair_block.shape
    triangle = jnp.einsum(
        "ikc,jkc->ijc",
        left_act,
        lax.all_gather(right_act, "row", axis=0, tiled=True),
        preferred_element_type=F32,
    )
    tnorm = layer_norm(triangle, out_gain).astype(BF16)
    swapped = lax.all_to_all(tnorm, "row", split_axis=1, concat_axis=0, tiled=True)
    normed_block = layer_norm(pair_block.astype(F32), in_gain).astype(BF16)
    gate_value = jax.nn.sigmoid(
        jnp.dot(normed_block.reshape(-1, channels), w_gate, preferred_element_type=F32)
    )
    outward = jnp.dot(swapped.reshape(-1, hidden), w_out, preferred_element_type=F32)
    return (gate_value * outward).reshape(block_rows, block_cols, channels).astype(BF16)


def sigmoid(value):
    return 0.5 * jnp.tanh(0.5 * value) + 0.5


def normed_rows(raw, gain, averaging):
    centered = raw.astype(F32) - jnp.dot(raw, averaging, preferred_element_type=F32)
    variance = jnp.dot((centered * centered).astype(BF16), averaging, preferred_element_type=F32)
    return (centered * lax.rsqrt(variance + 1e-05) * gain).astype(BF16)


def kernel(
    n,
    z_left_hbm, z_right_hbm, pair_hbm, row_valid_hbm, col_valid_hbm, k_valid_hbm,
    in_gain_hbm, w_left_hbm, w_right_hbm, w_gate_hbm, w_out_hbm, out_gain_hbm,
    out,
    z_left, z_right, pair, row_valid, col_valid, k_valid,
    in_gain, w_left, w_right, w_gate, w_out, out_gain,
    gathered, left, gate, partial, summing, outgoing, incoming,
    got, up_sem, down_sem, side_sem, twin_sem, back_sem, back_got, load_sem,
):
    rows, width, channels = z_left.shape
    cols = z_right.shape[0]
    per_block = rows * cols
    nz = n // 4
    me = lax.axis_index("row")
    core = lax.rem(me, 2)
    y = lax.rem(me // 2, 2)
    z = me // 4

    def place(pz, py, pc):
        return (pz * 2 + py) * 2 + pc

    loads = {}
    for index, (name, source, target) in enumerate((
        ("z_right", z_right_hbm, z_right),
        ("w_right", w_right_hbm, w_right),
        ("in_gain", in_gain_hbm, in_gain),
        ("k_valid", k_valid_hbm, k_valid),
        ("col_valid", col_valid_hbm, col_valid),
        ("z_left", z_left_hbm, z_left),
        ("w_left", w_left_hbm, w_left),
        ("row_valid", row_valid_hbm, row_valid),
        ("pair", pair_hbm, pair),
        ("w_gate", w_gate_hbm, w_gate),
        ("w_out", w_out_hbm, w_out),
        ("out_gain", out_gain_hbm, out_gain),
    )):
        loads[name] = pltpu.make_async_copy(source, target, load_sem.at[index])
        loads[name].start()

    barrier = pltpu.get_barrier_semaphore()

    def greet(step, _):
        peer = lax.rem(me + step, n)
        pl.semaphore_signal(barrier, inc=1, device_id={"row": peer}, device_id_type=MESH)
        return 0

    lax.fori_loop(1, n, greet, 0)

    def carry(src, chunk, sem, target):
        return pltpu.make_async_remote_copy(
            src_ref=gathered.at[src, chunk],
            dst_ref=gathered.at[src, chunk],
            send_sem=sem,
            recv_sem=got.at[src, chunk],
            device_id={"row": target},
            device_id_type=MESH,
        )

    def go_up(pz, chunk):
        return carry(place(pz, y, core), chunk, up_sem.at[pz, chunk], lax.rem(me + 4, n))

    def go_down(pz, chunk):
        return carry(place(pz, y, core), chunk, down_sem.at[pz, chunk], lax.rem(me + n - 4, n))

    def go_side(pz, chunk):
        return carry(place(pz, y, core), chunk, side_sem.at[pz, chunk], place(z, 1 - y, core))

    def go_twin(pz, py, chunk):
        return carry(
            place(pz, py, core), chunk, twin_sem.at[pz * 2 + py, chunk], place(z, y, 1 - core)
        )

    def give_back(src):
        return pltpu.make_async_remote_copy(
            src_ref=outgoing.at[src],
            dst_ref=incoming.at[me],
            send_sem=back_sem.at[src],
            recv_sem=back_got.at[me],
            device_id={"row": src},
            device_id_type=MESH,
        )

    def wait_got(src, chunk):
        carry(src, chunk, up_sem.at[0, 0], place(z, y, 1 - core)).wait_recv()

    for name in ("z_right", "w_right", "in_gain", "k_valid", "col_valid"):
        loads[name].wait()
    averaging = jnp.full((channels, channels), 1.0 / channels, BF16)
    gain = in_gain[...]

    across = lax.broadcasted_iota(jnp.int32, (width, width), 0)
    along = lax.broadcasted_iota(jnp.int32, (width, width), 1)
    spread = jnp.where(across == along, k_valid[...].astype(F32), 0.0).astype(BF16)
    k_mask = jnp.dot(spread, jnp.ones((width, channels), BF16), preferred_element_type=F32)

    for chunk in range(cols):
        projected = jnp.dot(
            normed_rows(z_right[chunk], gain, averaging), w_right[...], preferred_element_type=F32
        )
        valid = col_valid[chunk].astype(F32)
        gathered[me, chunk] = (
            sigmoid(projected[:, :channels]) * projected[:, channels:] * (k_mask * valid)
        ).astype(BF16)
        if chunk == 0:
            pl.semaphore_wait(barrier, n - 1)

        @pl.when(z + 1 < nz)
        def _():
            go_up(z, chunk).start()

        @pl.when(z > 0)
        def _():
            go_down(z, chunk).start()

        go_side(z, chunk).start()
        go_twin(z, y, chunk).start()

    for name in ("z_left", "w_left", "row_valid", "pair", "w_gate", "w_out", "out_gain"):
        loads[name].wait()

    def left_rows(quarter):
        def one(step, _):
            i = quarter * (rows // cols) + step
            projected = jnp.dot(
                normed_rows(z_left[i], gain, averaging), w_left[...], preferred_element_type=F32
            )
            valid = row_valid[i].astype(F32)
            left[i] = (
                sigmoid(projected[:, :channels]) * projected[:, channels:] * valid
            ).astype(BF16)
            return 0

        lax.fori_loop(0, rows // cols, one, 0)

    def gate_rows(quarter):
        size = pair.shape[0] // cols
        span = pl.ds(pl.multiple_of(quarter * size, size), size)
        normed = normed_rows(pair[span, :], gain, averaging)
        gate[span, :] = sigmoid(jnp.dot(normed, w_gate[...], preferred_element_type=F32))

    depth = 32
    pick_row = lax.broadcasted_iota(jnp.int32, (per_block, per_block * depth), 0)
    pick_col = lax.broadcasted_iota(jnp.int32, (per_block, per_block * depth), 1)
    summing[...] = (pick_col // depth == pick_row).astype(BF16)
    group = 2

    def triangle_block(src):
        def some_rows(at, _):
            totals = [[] for _ in range(group * cols)]
            for part in range(width // depth):
                span = pl.ds(part * depth, depth)
                rights = [gathered[src, j, span, :] for j in range(cols)]
                for ii in range(group):
                    one_left = left[at * group + ii, span, :]
                    for j in range(cols):
                        pile = totals[ii * cols + j]
                        term, level = one_left * rights[j], 0
                        while pile and pile[-1][1] == level:
                            term, level = pile.pop()[0] + term, level + 1
                        pile.append((term, level))
            for index, pile in enumerate(totals):
                total = pile.pop()[0]
                while pile:
                    total = pile.pop()[0] + total
                first = pl.multiple_of((at * group * cols + index) * depth, depth)
                partial[pl.ds(first, depth), :] = total
            return 0

        lax.fori_loop(0, rows // group, some_rows, 0)
        triangle = jnp.dot(summing[...], partial[...], preferred_element_type=F32)
        centered = triangle - jnp.mean(triangle, axis=-1, keepdims=True)
        variance = jnp.mean(centered * centered, axis=-1, keepdims=True)
        tnorm = (centered * lax.rsqrt(variance + 1e-05) * out_gain[...]).astype(BF16)
        outward = jnp.dot(tnorm, w_out[...], preferred_element_type=F32).astype(BF16)

        @pl.when(src == me)
        def _():
            incoming[me] = outward

        @pl.when(src != me)
        def _():
            outgoing[src] = outward
            give_back(src).start()

    def step(t, _):
        distance = t // cols
        chunk = lax.rem(t, cols)

        def arrivals(way, _):
            sign = 1 - 2 * way
            pz = z + (distance + 1) * sign

            @pl.when((pz >= 0) & (pz < nz))
            def _():
                wait_got(place(pz, y, core), chunk)

                @pl.when((way == 0) & (z > 0))
                def _():
                    go_down(pz, chunk).start()

                @pl.when((way == 1) & (z + 1 < nz))
                def _():
                    go_up(pz, chunk).start()

                go_side(pz, chunk).start()
                go_twin(pz, y, chunk).start()

            qz = z + distance * sign

            @pl.when((qz >= 0) & (qz < nz) & ((distance > 0) | (way == 0)))
            def _():
                wait_got(place(qz, 1 - y, core), chunk)
                go_twin(qz, 1 - y, chunk).start()

            return 0

        lax.fori_loop(0, 2, arrivals, 0)

        @pl.when(distance == 0)
        def _():
            left_rows(chunk)

        @pl.when(distance == 1)
        def _():
            gate_rows(chunk)

        def blocks(way, _):
            before = distance - 1
            pz = z + before * (1 - 2 * way)
            across_y = lax.rem(chunk, 2)
            across_core = chunk // 2

            @pl.when((pz >= 0) & (pz < nz) & ((before > 0) | ((before == 0) & (way == 0))))
            def _():
                py = lax.rem(y + across_y, 2)
                src = place(pz, py, lax.rem(core + across_core, 2))

                @pl.when(across_core == 1)
                def _():
                    for c in range(cols):
                        wait_got(src, c)

                triangle_block(src)

            return 0

        lax.fori_loop(0, 2, blocks, 0)
        return 0

    lax.fori_loop(0, (nz + 1) * cols, step, 0)

    def finish(src, _):
        @pl.when(src != me)
        def _():
            pltpu.make_async_remote_copy(
                src_ref=outgoing.at[src],
                dst_ref=incoming.at[src],
                send_sem=back_sem.at[src],
                recv_sem=back_got.at[src],
                device_id={"row": src},
                device_id_type=MESH,
            ).wait_recv()

        span = pl.ds(pl.multiple_of(src * per_block, per_block), per_block)
        out[span, :] = (gate[span, :] * incoming[src].astype(F32)).astype(BF16)
        return 0

    lax.fori_loop(0, n, finish, 0)

    def settle(pz, _):
        for chunk in range(cols):
            @pl.when((pz <= z) & (z + 1 < nz))
            def _():
                go_up(pz, chunk).wait_send()

            @pl.when((pz >= z) & (z > 0))
            def _():
                go_down(pz, chunk).wait_send()

            go_side(pz, chunk).wait_send()
            go_twin(pz, 0, chunk).wait_send()
            go_twin(pz, 1, chunk).wait_send()
        return 0

    lax.fori_loop(0, nz, settle, 0)

    def settle_back(src, _):
        @pl.when(src != me)
        def _():
            give_back(src).wait_send()

        return 0

    lax.fori_loop(0, n, settle_back, 0)


def local_kernel(
    n,
    z_left, z_right, pair_block, row_valid, col_valid, k_valid,
    in_gain, w_left, w_right, w_gate, w_out, out_gain,
):
    rows, width, channels = z_left.shape
    cols = z_right.shape[0]
    per_block = rows * cols
    nz = n // 4
    dma = pltpu.SemaphoreType.DMA
    flat = pl.pallas_call(
        functools.partial(kernel, n),
        out_shape=jax.ShapeDtypeStruct((n * per_block, channels), BF16),
        in_specs=[pl.BlockSpec(memory_space=pl.ANY)] * 12,
        out_specs=pl.BlockSpec(memory_space=pltpu.VMEM),
        scratch_shapes=[
            pltpu.VMEM(z_left.shape, BF16),
            pltpu.VMEM(z_right.shape, BF16),
            pltpu.VMEM((n * per_block, channels), BF16),
            pltpu.SMEM(row_valid.shape, jnp.int32),
            pltpu.SMEM(col_valid.shape, jnp.int32),
            pltpu.VMEM((1, width), jnp.int32),
            pltpu.VMEM((1, channels), F32),
            pltpu.VMEM(w_left.shape, BF16),
            pltpu.VMEM(w_right.shape, BF16),
            pltpu.VMEM(w_gate.shape, BF16),
            pltpu.VMEM(w_out.shape, BF16),
            pltpu.VMEM((1, channels), F32),
            pltpu.VMEM((n, cols, width, channels), BF16),
            pltpu.VMEM((rows, width, channels), BF16),
            pltpu.VMEM((n * per_block, channels), F32),
            pltpu.VMEM((per_block * 32, channels), BF16),
            pltpu.VMEM((per_block, per_block * 32), BF16),
            pltpu.VMEM((n, per_block, channels), BF16),
            pltpu.VMEM((n, per_block, channels), BF16),
            dma((n, cols)),
            dma((nz, cols)),
            dma((nz, cols)),
            dma((nz, cols)),
            dma((nz * 2, cols)),
            dma((n,)),
            dma((n,)),
            dma((12,)),
        ],
        compiler_params=pltpu.CompilerParams(
            collective_id=0, has_side_effects=True, vmem_limit_bytes=60 * 1024 * 1024
        ),
    )(
        z_left, z_right, pair_block.reshape(-1, channels), row_valid, col_valid,
        k_valid.reshape(1, -1), in_gain.reshape(1, -1), w_left, w_right, w_gate, w_out,
        out_gain.reshape(1, -1),
    )
    return flat.reshape(pair_block.shape)


def fits(n, z_left, z_right):
    rows, width, channels = z_left.shape
    cols = z_right.shape[0]
    return (
        n % 4 == 0
        and cols == 4
        and rows % 4 == 0
        and width % 32 == 0
        and n * cols * width * channels * 2 <= 8 * 1024 * 1024
    )


def solution(mesh):
    n = mesh.shape["row"]

    def local(*arrays):
        if fits(n, arrays[0], arrays[1]):
            return local_kernel(n, *arrays)
        return local_collectives(*arrays)

    placed = (
        P(("parts", "row"), None, None),
        P(("parts", "row"), None, None),
        P("parts", "row", None),
        P(("parts", "row")),
        P(("parts", "row")),
        P("parts"),
        P(),
        P(),
        P(),
        P(),
        P(),
        P(),
    )
    return jax.shard_map(
        local, mesh=mesh, in_specs=placed, out_specs=P("parts", "row", None), check_vma=False
    )
```

```python
import functools

import jax
import jax.numpy as jnp
from jax import lax
from jax.experimental import pallas as pl
from jax.experimental.pallas import tpu as pltpu
from jax.sharding import PartitionSpec as P

MESH = pl.DeviceIdType.MESH
F32 = jnp.float32
BF16 = jnp.bfloat16


def layer_norm(values, scale_gain):
    average = jnp.mean(values, axis=-1, keepdims=True)
    centered = values - average
    variance = jnp.mean(centered * centered, axis=-1, keepdims=True)
    return centered / jnp.sqrt(variance + 1e-05) * scale_gain


def activations(raw_pairs, valid_rows, k_valid, in_gain, weight):
    row_count, width_k, channels = raw_pairs.shape
    normed = layer_norm(raw_pairs.astype(F32), in_gain).astype(BF16)
    projected = jnp.dot(
        normed.reshape(row_count * width_k, channels), weight, preferred_element_type=F32
    )
    projected = projected.reshape(row_count, width_k, -1)
    hidden = projected.shape[-1] // 2
    masking = valid_rows.astype(F32)[:, None] * k_valid.astype(F32)[None, :]
    return (
        jax.nn.sigmoid(projected[..., :hidden]) * projected[..., hidden:] * masking[..., None]
    ).astype(BF16)


def local_collectives(
    z_left, z_right, pair_block, row_valid, col_valid, k_valid,
    in_gain, w_left, w_right, w_gate, w_out, out_gain,
):
    left_act = activations(z_left, row_valid, k_valid, in_gain, w_left)
    right_act = activations(z_right, col_valid, k_valid, in_gain, w_right)
    hidden = left_act.shape[2]
    block_rows, block_cols, channels = pair_block.shape
    triangle = jnp.einsum(
        "ikc,jkc->ijc",
        left_act,
        lax.all_gather(right_act, "row", axis=0, tiled=True),
        preferred_element_type=F32,
    )
    tnorm = layer_norm(triangle, out_gain).astype(BF16)
    swapped = lax.all_to_all(tnorm, "row", split_axis=1, concat_axis=0, tiled=True)
    normed_block = layer_norm(pair_block.astype(F32), in_gain).astype(BF16)
    gate_value = jax.nn.sigmoid(
        jnp.dot(normed_block.reshape(-1, channels), w_gate, preferred_element_type=F32)
    )
    outward = jnp.dot(swapped.reshape(-1, hidden), w_out, preferred_element_type=F32)
    return (gate_value * outward).reshape(block_rows, block_cols, channels).astype(BF16)


def sigmoid(value):
    return 0.5 * jnp.tanh(0.5 * value) + 0.5


def normed_rows(raw, gain, averaging):
    centered = raw.astype(F32) - jnp.dot(raw, averaging, preferred_element_type=F32)
    variance = jnp.dot((centered * centered).astype(BF16), averaging, preferred_element_type=F32)
    return (centered * lax.rsqrt(variance + 1e-05) * gain).astype(BF16)


def kernel(
    n,
    z_left_hbm, z_right_hbm, pair_hbm, row_valid_hbm, col_valid_hbm, k_valid_hbm,
    in_gain_hbm, w_left_hbm, w_right_hbm, w_gate_hbm, w_out_hbm, out_gain_hbm,
    out,
    z_left, z_right, pair, row_valid, col_valid, k_valid,
    in_gain, w_left, w_right, w_gate, w_out, out_gain,
    gathered, left, gate, partial, summing, outgoing, incoming,
    got, up_sem, down_sem, side_sem, twin_sem, back_sem, back_got, load_sem,
):
    rows, width, channels = z_left.shape
    cols = z_right.shape[0]
    per_block = rows * cols
    nz = n // 4
    me = lax.axis_index("row")
    core = lax.rem(me, 2)
    y = lax.rem(me // 2, 2)
    z = me // 4

    def place(pz, py, pc):
        return (pz * 2 + py) * 2 + pc

    loads = {}
    for index, (name, source, target) in enumerate((
        ("z_right", z_right_hbm, z_right),
        ("w_right", w_right_hbm, w_right),
        ("in_gain", in_gain_hbm, in_gain),
        ("k_valid", k_valid_hbm, k_valid),
        ("col_valid", col_valid_hbm, col_valid),
        ("z_left", z_left_hbm, z_left),
        ("w_left", w_left_hbm, w_left),
        ("row_valid", row_valid_hbm, row_valid),
        ("pair", pair_hbm, pair),
        ("w_gate", w_gate_hbm, w_gate),
        ("w_out", w_out_hbm, w_out),
        ("out_gain", out_gain_hbm, out_gain),
    )):
        loads[name] = pltpu.make_async_copy(source, target, load_sem.at[index])
        loads[name].start()

    barrier = pltpu.get_barrier_semaphore()

    def greet(step, _):
        peer = lax.rem(me + step, n)
        pl.semaphore_signal(barrier, inc=1, device_id={"row": peer}, device_id_type=MESH)
        return 0

    lax.fori_loop(1, n, greet, 0)

    def carry(src, chunk, sem, target):
        return pltpu.make_async_remote_copy(
            src_ref=gathered.at[src, chunk],
            dst_ref=gathered.at[src, chunk],
            send_sem=sem,
            recv_sem=got.at[src, chunk],
            device_id={"row": target},
            device_id_type=MESH,
        )

    def go_up(pz, chunk):
        return carry(place(pz, y, core), chunk, up_sem.at[pz, chunk], lax.rem(me + 4, n))

    def go_down(pz, chunk):
        return carry(place(pz, y, core), chunk, down_sem.at[pz, chunk], lax.rem(me + n - 4, n))

    def go_side(pz, chunk):
        return carry(place(pz, y, core), chunk, side_sem.at[pz, chunk], place(z, 1 - y, core))

    def go_twin(pz, py, chunk):
        return carry(
            place(pz, py, core), chunk, twin_sem.at[pz * 2 + py, chunk], place(z, y, 1 - core)
        )

    def give_back(src):
        return pltpu.make_async_remote_copy(
            src_ref=outgoing.at[src],
            dst_ref=incoming.at[me],
            send_sem=back_sem.at[src],
            recv_sem=back_got.at[me],
            device_id={"row": src},
            device_id_type=MESH,
        )

    def wait_got(src, chunk):
        carry(src, chunk, up_sem.at[0, 0], place(z, y, 1 - core)).wait_recv()

    for name in ("z_right", "w_right", "in_gain", "k_valid", "col_valid"):
        loads[name].wait()
    averaging = jnp.full((channels, channels), 1.0 / channels, BF16)
    gain = in_gain[...]

    across = lax.broadcasted_iota(jnp.int32, (width, width), 0)
    along = lax.broadcasted_iota(jnp.int32, (width, width), 1)
    spread = jnp.where(across == along, k_valid[...].astype(F32), 0.0).astype(BF16)
    k_mask = jnp.dot(spread, jnp.ones((width, channels), BF16), preferred_element_type=F32)

    for chunk in range(cols):
        projected = jnp.dot(
            normed_rows(z_right[chunk], gain, averaging), w_right[...], preferred_element_type=F32
        )
        valid = col_valid[chunk].astype(F32)
        gathered[me, chunk] = (
            sigmoid(projected[:, :channels]) * projected[:, channels:] * (k_mask * valid)
        ).astype(BF16)
        if chunk == 0:
            pl.semaphore_wait(barrier, n - 1)

        @pl.when(z + 1 < nz)
        def _():
            go_up(z, chunk).start()

        @pl.when(z > 0)
        def _():
            go_down(z, chunk).start()

        go_side(z, chunk).start()
        go_twin(z, y, chunk).start()

    for name in ("z_left", "w_left", "row_valid", "pair", "w_gate", "w_out", "out_gain"):
        loads[name].wait()

    def left_rows(quarter):
        def one(step, _):
            i = quarter * (rows // cols) + step
            projected = jnp.dot(
                normed_rows(z_left[i], gain, averaging), w_left[...], preferred_element_type=F32
            )
            valid = row_valid[i].astype(F32)
            left[i] = (
                sigmoid(projected[:, :channels]) * projected[:, channels:] * valid
            ).astype(BF16)
            return 0

        lax.fori_loop(0, rows // cols, one, 0)

    def gate_rows(quarter):
        size = pair.shape[0] // cols
        span = pl.ds(pl.multiple_of(quarter * size, size), size)
        normed = normed_rows(pair[span, :], gain, averaging)
        gate[span, :] = sigmoid(jnp.dot(normed, w_gate[...], preferred_element_type=F32))

    depth = 32
    pick_row = lax.broadcasted_iota(jnp.int32, (per_block, per_block * depth), 0)
    pick_col = lax.broadcasted_iota(jnp.int32, (per_block, per_block * depth), 1)
    summing[...] = (pick_col // depth == pick_row).astype(BF16)
    group = 2

    def triangle_pair(first, second):
        pair_of = (first, second)

        def some_rows(at, _):
            totals = [None] * (group * 2 * cols)
            for part in range(0, width // depth, 2):
                spans = [pl.ds((part + half) * depth, depth) for half in range(2)]
                lefts = [[left[at * group + ii, span, :] for span in spans] for ii in range(group)]
                for which, src in enumerate(pair_of):
                    for j in range(cols):
                        rights = [gathered[src, j, span, :] for span in spans]
                        for ii in range(group):
                            index = (which * group + ii) * cols + j
                            term = lefts[ii][0] * rights[0] + lefts[ii][1] * rights[1]
                            held = totals[index]
                            totals[index] = term if held is None else held + term
            for which in range(2):
                for index in range(group * cols):
                    place_at = pl.multiple_of((at * group * cols + index) * depth, depth)
                    partial[which, pl.ds(place_at, depth), :] = totals[which * group * cols + index]
            return 0

        lax.fori_loop(0, rows // group, some_rows, 0)
        triangle = jnp.concatenate(
            [
                jnp.dot(summing[...], partial[which], preferred_element_type=F32)
                for which in range(2)
            ],
            axis=0,
        )
        centered = triangle - jnp.mean(triangle, axis=-1, keepdims=True)
        variance = jnp.mean(centered * centered, axis=-1, keepdims=True)
        tnorm = (centered * lax.rsqrt(variance + 1e-05) * out_gain[...]).astype(BF16)
        outward = jnp.dot(tnorm, w_out[...], preferred_element_type=F32).astype(BF16)

        @pl.when(first == me)
        def _():
            incoming[me] = outward[:per_block]

        @pl.when(first != me)
        def _():
            outgoing[first] = outward[:per_block]
            give_back(first).start()

        outgoing[second] = outward[per_block:]
        give_back(second).start()

    def step(t, _):
        distance = t // cols
        chunk = lax.rem(t, cols)

        def arrivals(way, _):
            sign = 1 - 2 * way
            pz = z + (distance + 1) * sign

            @pl.when((pz >= 0) & (pz < nz))
            def _():
                wait_got(place(pz, y, core), chunk)

                @pl.when((way == 0) & (z > 0))
                def _():
                    go_down(pz, chunk).start()

                @pl.when((way == 1) & (z + 1 < nz))
                def _():
                    go_up(pz, chunk).start()

                go_side(pz, chunk).start()
                go_twin(pz, y, chunk).start()

            qz = z + distance * sign

            @pl.when((qz >= 0) & (qz < nz) & ((distance > 0) | (way == 0)))
            def _():
                wait_got(place(qz, 1 - y, core), chunk)
                go_twin(qz, 1 - y, chunk).start()

            return 0

        lax.fori_loop(0, 2, arrivals, 0)

        @pl.when(distance == 0)
        def _():
            left_rows(chunk)

        @pl.when(distance == 1)
        def _():
            gate_rows(chunk)

        late = (chunk < 2).astype(jnp.int32)
        far = distance - late
        way = lax.rem(chunk, 2)
        own = ((far == 0) & (way == 1)).astype(jnp.int32)
        pz = z + far * (1 - 2 * way)
        py = lax.rem(y + late * (1 - own), 2)

        @pl.when((distance > 0) & (pz >= 0) & (pz < nz))
        def _():
            first = place(pz, py, core)
            second = place(pz, py, 1 - core)
            for c in range(cols):
                wait_got(second, c)
            triangle_pair(first, second)

        return 0

    lax.fori_loop(0, nz * cols + 2, step, 0)

    def finish(src, _):
        @pl.when(src != me)
        def _():
            pltpu.make_async_remote_copy(
                src_ref=outgoing.at[src],
                dst_ref=incoming.at[src],
                send_sem=back_sem.at[src],
                recv_sem=back_got.at[src],
                device_id={"row": src},
                device_id_type=MESH,
            ).wait_recv()

        span = pl.ds(pl.multiple_of(src * per_block, per_block), per_block)
        out[span, :] = (gate[span, :] * incoming[src].astype(F32)).astype(BF16)
        return 0

    lax.fori_loop(0, n, finish, 0)

    def settle(pz, _):
        for chunk in range(cols):
            @pl.when((pz <= z) & (z + 1 < nz))
            def _():
                go_up(pz, chunk).wait_send()

            @pl.when((pz >= z) & (z > 0))
            def _():
                go_down(pz, chunk).wait_send()

            go_side(pz, chunk).wait_send()
            go_twin(pz, 0, chunk).wait_send()
            go_twin(pz, 1, chunk).wait_send()
        return 0

    lax.fori_loop(0, nz, settle, 0)

    def settle_back(src, _):
        @pl.when(src != me)
        def _():
            give_back(src).wait_send()

        return 0

    lax.fori_loop(0, n, settle_back, 0)


def local_kernel(
    n,
    z_left, z_right, pair_block, row_valid, col_valid, k_valid,
    in_gain, w_left, w_right, w_gate, w_out, out_gain,
):
    rows, width, channels = z_left.shape
    cols = z_right.shape[0]
    per_block = rows * cols
    nz = n // 4
    dma = pltpu.SemaphoreType.DMA
    flat = pl.pallas_call(
        functools.partial(kernel, n),
        out_shape=jax.ShapeDtypeStruct((n * per_block, channels), BF16),
        in_specs=[pl.BlockSpec(memory_space=pl.ANY)] * 12,
        out_specs=pl.BlockSpec(memory_space=pltpu.VMEM),
        scratch_shapes=[
            pltpu.VMEM(z_left.shape, BF16),
            pltpu.VMEM(z_right.shape, BF16),
            pltpu.VMEM((n * per_block, channels), BF16),
            pltpu.SMEM(row_valid.shape, jnp.int32),
            pltpu.SMEM(col_valid.shape, jnp.int32),
            pltpu.VMEM((1, width), jnp.int32),
            pltpu.VMEM((1, channels), F32),
            pltpu.VMEM(w_left.shape, BF16),
            pltpu.VMEM(w_right.shape, BF16),
            pltpu.VMEM(w_gate.shape, BF16),
            pltpu.VMEM(w_out.shape, BF16),
            pltpu.VMEM((1, channels), F32),
            pltpu.VMEM((n, cols, width, channels), BF16),
            pltpu.VMEM((rows, width, channels), BF16),
            pltpu.VMEM((n * per_block, channels), F32),
            pltpu.VMEM((2, per_block * 32, channels), BF16),
            pltpu.VMEM((per_block, per_block * 32), BF16),
            pltpu.VMEM((n, per_block, channels), BF16),
            pltpu.VMEM((n, per_block, channels), BF16),
            dma((n, cols)),
            dma((nz, cols)),
            dma((nz, cols)),
            dma((nz, cols)),
            dma((nz * 2, cols)),
            dma((n,)),
            dma((n,)),
            dma((12,)),
        ],
        compiler_params=pltpu.CompilerParams(
            collective_id=0, has_side_effects=True, vmem_limit_bytes=60 * 1024 * 1024
        ),
    )(
        z_left, z_right, pair_block.reshape(-1, channels), row_valid, col_valid,
        k_valid.reshape(1, -1), in_gain.reshape(1, -1), w_left, w_right, w_gate, w_out,
        out_gain.reshape(1, -1),
    )
    return flat.reshape(pair_block.shape)


def fits(n, z_left, z_right):
    rows, width, channels = z_left.shape
    cols = z_right.shape[0]
    return (
        n % 4 == 0
        and cols == 4
        and rows % 4 == 0
        and width % 32 == 0
        and n * cols * width * channels * 2 <= 8 * 1024 * 1024
    )


def solution(mesh):
    n = mesh.shape["row"]

    def local(*arrays):
        if fits(n, arrays[0], arrays[1]):
            return local_kernel(n, *arrays)
        return local_collectives(*arrays)

    placed = (
        P(("parts", "row"), None, None),
        P(("parts", "row"), None, None),
        P("parts", "row", None),
        P(("parts", "row")),
        P(("parts", "row")),
        P("parts"),
        P(),
        P(),
        P(),
        P(),
        P(),
        P(),
    )
    return jax.shard_map(
        local, mesh=mesh, in_specs=placed, out_specs=P("parts", "row", None), check_vma=False
    )
```
